32 devices in a mesh: tiles: 2 (over y), band: 4 (over x, core), head: 4 (over z).
Axes of the slice: x: 2, y: 2, z: 4, core: 2. Of those that a mesh axis runs over, the one named last changes fastest.
Arguments:
- tokens: bfloat16 [8192, 1024], P(('tiles', 'band')), parts along dimension 0, may hold values from -24 to 24
- w_query: bfloat16 [1024, 1024], P(None, 'head'), may hold values from -0.375 to 0.375
- w_key: bfloat16 [1024, 1024], P(None, 'head'), may hold values from -0.1875 to 0.1875
- w_value: bfloat16 [1024, 1024], P(None, 'head'), may hold values from -0.1875 to 0.1875
- w_out: bfloat16 [1024, 1024], P('head'), may hold values from -0.75 to 0.75
- block_mask: int32 [64, 32], P('tiles'), parts along dimension 0, may hold values from 0 to 1, as said below
Outputs:
- projected: bfloat16 [8192, 1024], P(('tiles', 'band', 'head')), parts along dimension 0
The draws below stay inside these ranges and needn't reach their ends.
There are 2 independent parts, one for each index of `tiles`. The reference program is written for one: setup_inputs(seed, part) draws one part's arguments, and reference() takes and returns one part's arrays. A program takes and returns all parts, laid end to end along the dimension named above; an argument that names none is the same for every part. Nothing has to cross between parts.
Inputs may be any that keep to these rules, and one draw needn't show every extreme that they name: `block_mask`: entries are 0 or 1. Every query block may attend to at least one key block. Among the 8 key blocks of one band at most 6 are named by some query block, and some band has exactly 6.
All inputs are finite; a program needn't handle non-finite values.
Results may differ from the reference program's by a relative error of at most 0.02.
Values may be sent and summed in bfloat16 or wider, within the bound.
A program may use at most 128 MiB of HBM per device.

```python
import math
import jax
import jax.numpy as jnp
from jax import lax

D = 1024
HEADS = 16
HD = 64
BLK = 128
TOK_DEV = 1024
TOKENS = 4096
KEEP = 6


def draw_tokens(key, part):
    first, second = jax.random.split(key, 2)
    base = jax.random.truncated_normal(first, -4.0, 4.0, (TOKENS, D), jnp.float32)
    row_scale = jnp.exp(jax.random.uniform(second, (TOKENS, 1), jnp.float32, math.log(0.7), math.log(1.4)))
    return (base * row_scale).astype(jnp.bfloat16)


def draw_block_mask(key, part):
    block_total = TOKENS // BLK
    per_band = TOK_DEV // BLK
    band_total = TOKENS // TOK_DEV
    streams = jax.random.split(key, 7)
    lowest = (KEEP + 1) // 2
    kept_counts = jax.random.randint(streams[0], (band_total,), lowest, KEEP + 1)
    forced = jax.random.randint(streams[1], (), 0, band_total)
    kept_counts = jnp.where(jnp.arange(band_total) == forced, KEEP, kept_counts)
    raw_order = jax.random.randint(streams[2], (band_total, per_band), 0, 1 << 20) * per_band + jnp.arange(per_band)[None, :]
    block_ranks = jnp.argsort(jnp.argsort(raw_order, axis=1), axis=1)
    has_data = (block_ranks < kept_counts[:, None]).reshape(block_total).astype(jnp.int32)
    levels = jax.random.randint(streams[3], (band_total,), 0, 8)
    percent = 4 + 88 * levels * levels // 49
    band_of_row = jnp.arange(block_total) // per_band
    chance = jax.random.randint(streams[4], (block_total, block_total), 0, 100)
    allowed = (chance < percent[band_of_row][:, None]).astype(jnp.int32) * has_data[None, :]
    pick_raw = (jax.random.randint(streams[5], (block_total, block_total), 0, 1 << 16) * block_total + jnp.arange(block_total)[None, :] + 1) * has_data[None, :]
    picked = jnp.argmax(pick_raw, axis=1)
    allowed = jnp.maximum(allowed, (jnp.arange(block_total)[None, :] == picked[:, None]).astype(jnp.int32))
    row_pick = jax.random.randint(streams[6], (block_total,), 0, block_total)
    column_hits = (jnp.arange(block_total)[:, None] == row_pick[None, :]).astype(jnp.int32) * has_data[None, :]
    allowed = jnp.maximum(allowed, column_hits)
    return allowed.astype(jnp.int32)


def block_levels(stream_key, shape, shards, low, high):
    def one(dim, blocks):
        draws = jax.random.uniform(jax.random.fold_in(jax.random.fold_in(stream_key, 6), dim), (blocks,), jnp.float32, low / len(shards), high / len(shards))
        return jnp.repeat(jnp.exp(draws), shape[dim] // blocks).reshape((-1,) + (1,) * (len(shape) - dim - 1))

    level = one(*shards[0])
    for cut in shards[1:]:
        level = level * one(*cut)
    return level


def scatter_about(rng, dims, width, reach, cuts=(), held_as=jnp.bfloat16):
    level = block_levels(rng, dims, cuts, -0.22, 0.18) if cuts else 1.0
    array = jax.random.normal(rng, dims, jnp.float32) * width * level
    return jnp.minimum(jnp.maximum(array, -reach), reach).astype(held_as)


def setup_inputs(seed: int = 0, part: int = 0) -> dict:
    seeds = jax.random.split(jax.random.key(seed), 7)
    own_keys = jax.random.split(jax.random.fold_in(seeds[6], part), 7)
    return {
        "tokens": draw_tokens(jax.random.fold_in(jax.random.fold_in(seeds[6], part), 71), part),
        "w_query": scatter_about(seeds[1], (D, D), (D // 4) ** -0.5, 0.375, ((1, 4),)),
        "w_key": scatter_about(seeds[2], (D, D), D ** -0.5, 0.1875, ((1, 4),)),
        "w_value": scatter_about(seeds[3], (D, D), D ** -0.5, 0.1875, ((1, 4),)),
        "w_out": scatter_about(seeds[4], (D, D), HD ** -0.5, 0.75, ((0, 4),)),
        "block_mask": draw_block_mask(jax.random.fold_in(jax.random.fold_in(seeds[6], part), 71), part),
    }


def reference(tokens, w_query, w_key, w_value, w_out, block_mask):
    queries = jnp.dot(tokens, w_query, preferred_element_type=jnp.float32).astype(jnp.bfloat16)
    key_rows = jnp.dot(tokens, w_key, preferred_element_type=jnp.float32).astype(jnp.bfloat16)
    value_rows = jnp.dot(tokens, w_value, preferred_element_type=jnp.float32).astype(jnp.bfloat16)
    total_rows = tokens.shape[0]
    block_count = total_rows // BLK
    key_heads = key_rows.astype(jnp.float32).reshape(total_rows, HEADS, HD)
    value_heads = value_rows.astype(jnp.float32).reshape(total_rows, HEADS, HD)
    score_scale = HD ** -0.5

    def one_block(packed):
        query_block, mask_row = packed
        query_heads = query_block.astype(jnp.float32).reshape(BLK, HEADS, HD)
        scores = jnp.einsum("rhd,khd->hrk", query_heads, key_heads, precision=lax.Precision.HIGHEST) * score_scale
        keep_keys = jnp.repeat(mask_row, BLK) > 0
        scores = jnp.where(keep_keys[None, None, :], scores, -jnp.inf)
        row_peak = jnp.max(scores, axis=2, keepdims=True)
        exponent = jnp.where(keep_keys[None, None, :], jnp.exp(scores - row_peak), 0.0)
        row_mass = jnp.sum(exponent, axis=2)
        rounded = lax.optimization_barrier(exponent.astype(jnp.bfloat16)).astype(jnp.float32)
        weighted = jnp.einsum("hrk,khd->rhd", rounded, value_heads, precision=lax.Precision.HIGHEST)
        return (weighted / row_mass.T[:, :, None]).reshape(BLK, HEADS * HD).astype(jnp.bfloat16)

    attended = lax.map(one_block, (queries.reshape(block_count, BLK, HEADS * HD), block_mask))
    attended = attended.reshape(total_rows, HEADS * HD)
    return jnp.dot(attended, w_out, preferred_element_type=jnp.float32).astype(jnp.bfloat16)
```

```python
import functools
import jax
import jax.numpy as jnp
from jax import lax
from jax.experimental import pallas as pl
from jax.experimental.pallas import tpu as pltpu
from jax.sharding import PartitionSpec as P

HD = 64
BLK = 128
KEEP = 6
LOW = -float(2**100)
SCALE = HD**-0.5 * 1.4426950408889634
MIB = 1 << 20
BF16 = jnp.bfloat16
F32 = jnp.float32
I32 = jnp.int32
NT = (((1,), (1,)), ((), ()))
W = KEEP * BLK


def select_blocks(mask, me, per_band):
    named = []
    for i in range(per_band):
        named.append(
            functools.reduce(jnp.maximum, [mask[r, me * per_band + i] for r in range(mask.shape[0])])
        )
    picks, rank = [0] * KEEP, 0
    for i in range(per_band):
        for k in range(min(i + 1, KEEP)):
            picks[k] = picks[k] + i * named[i] * (rank == k)
        rank = rank + named[i]
    return picks


def make_bias(mask, me, nb, bias):
    n_rows, n_kb = mask.shape
    nq = n_kb // nb
    slots = bias.shape[1]
    everything = mask[...].astype(F32).T
    rows = mask[pl.ds(pl.multiple_of(me * nq, nq), nq), :].astype(F32)
    named = jnp.broadcast_to(jnp.max(everything, axis=1, keepdims=True), (n_kb, slots))
    left = lax.broadcasted_iota(I32, (n_kb, n_kb), 0)
    right = lax.broadcasted_iota(I32, (n_kb, n_kb), 1)
    earlier = ((right < left) & (left // nq == right // nq)).astype(F32)
    rank = jnp.dot(earlier, named, preferred_element_type=F32)
    band = (lax.broadcasted_iota(I32, (n_kb, slots), 0) // nq).astype(F32)
    slot = lax.broadcasted_iota(I32, (n_kb, slots), 1).astype(F32)
    place = jnp.where((slot == band * KEEP + rank) & (named > 0) & (rank < KEEP), 1.0, 0.0)
    allowed = jnp.dot(rows, place, preferred_element_type=F32)
    value = jnp.where(allowed > 0, 0.0, LOW)
    for i in range(nq):
        bias[i * BLK : (i + 1) * BLK, :] = jnp.broadcast_to(value[i : i + 1, :], (BLK, slots)).astype(BF16)


def layer(
    nt, nb, nz, mask_h, tok_h, wq_h, wk_h, wv_h, wo_h, out,
    mask_s, mask_v, tok, wq, wk, wv, rows_v, kv, q_pad, bias, onehot, top, acc, att, got, wo, pre,
    load, kv_send, kv_fwd, kv_recv, a_send, a_recv, w1_send, w2_send, w3_send, w_recv,
):
    nh = q_pad.shape[0]
    nq = tok.shape[0]
    n_chips = nb // 2
    slots = bias.shape[1]
    n_rows = nq * BLK
    depth = wo.shape[1]
    parts = 2 * nt
    per_part = depth // parts
    half = att.shape[2]
    tile, band, z = lax.axis_index("tiles"), lax.axis_index("band"), lax.axis_index("head")
    chip, core = band // 2, lax.rem(band, 2)
    sibling = chip * 2 + 1 - core
    mesh_id = pl.DeviceIdType.MESH

    pairs = ((mask_h, mask_s), (mask_h, mask_v), (tok_h, tok), (wk_h, wk), (wv_h, wv), (wq_h, wq), (wo_h, wo.at[z]))
    loads = [pltpu.make_async_copy(a, b, load.at[i]) for i, (a, b) in enumerate(pairs)]
    for c in loads:
        c.start()

    def chip_at(step):
        return lax.rem(chip + step, n_chips)

    peers = [{"band": sibling}]
    peers += [{"band": chip_at(d) * 2 + core} for d in range(1, n_chips)]
    peers += [{"head": lax.rem(z + d, nz)} for d in range(1, nz)]
    peers += [{"tiles": lax.rem(tile + d, nt)} for d in range(1, nt)]
    barrier = pltpu.get_barrier_semaphore()
    for p in peers:
        pl.semaphore_signal(barrier, inc=1, device_id=p, device_id_type=mesh_id)

    def remote(src, dst, send, recv, to):
        return pltpu.make_async_remote_copy(
            src_ref=src, dst_ref=dst, send_sem=send, recv_sem=recv, device_id=to, device_id_type=mesh_id
        )

    def kv_copy(h, origin, send, to):
        return remote(kv.at[h, origin], kv.at[h, origin], send, kv_recv.at[h, origin], {"band": to})

    def kv_direct(h, step):
        return kv_copy(h, band, kv_send.at[h, step], chip_at(step) * 2 + core)

    def kv_own(h):
        return kv_copy(h, band, kv_send.at[h, 0], sibling)

    def kv_forward(h, step):
        return kv_copy(h, chip_at(step) * 2 + core, kv_fwd.at[h, step], sibling)

    def kv_arrived(h, origin):
        kv_copy(h, origin, kv_recv.at[h, origin], sibling).wait_recv()

    def w_piece(source, part):
        return wo.at[source, pl.ds(pl.multiple_of(part * per_part, per_part), per_part)]

    my_part = tile * 2 + core

    def w_first(d):
        here = pl.ds(pl.multiple_of(my_part * per_part, per_part), per_part)
        return remote(
            wo_h.at[here], w_piece(z, my_part), w1_send.at[d], w_recv.at[z, my_part], {"head": lax.rem(z + d, nz)}
        )

    def w_second(d, t):
        source = lax.rem(z + d, nz)
        piece = w_piece(source, my_part)
        return remote(piece, piece, w2_send.at[d, t], w_recv.at[source, my_part], {"tiles": lax.rem(tile + t, nt)})

    def w_third(d, t):
        source, part = lax.rem(z + d, nz), lax.rem(tile + t, nt) * 2 + core
        piece = w_piece(source, part)
        return remote(piece, piece, w3_send.at[d, t], w_recv.at[source, part], {"band": sibling})

    def w_arrived(d, part):
        source = lax.rem(z + d, nz)
        piece = w_piece(source, part)
        remote(piece, piece, w1_send.at[d], w_recv.at[source, part], {"band": sibling}).wait_recv()

    slot_of = lax.broadcasted_iota(I32, (BLK, slots), 1)
    for s in range(nb * KEEP):
        onehot[s * BLK : (s + 1) * BLK, :] = jnp.where(slot_of == s, 1.0, 0.0).astype(BF16)
    loads[0].wait()
    sel = select_blocks(mask_s, band, nq)
    loads[1].wait()
    make_bias(mask_v, band, nb, bias)
    pl.semaphore_wait(barrier, len(peers))
    for d in range(1, nz):
        w_first(d).start()

    lane = lax.broadcasted_iota(I32, (1, BLK), 1)
    low_half = lane < HD

    loads[2].wait()
    for k in range(KEEP):
        rows_v[k * BLK : (k + 1) * BLK, :] = tok[sel[k]]
    loads[3].wait()
    loads[4].wait()
    for g in range(0, nh, 4):
        cols = slice(g * HD, min(g + 4, nh) * HD)
        keys = jnp.dot(rows_v[...], wk[:, cols], preferred_element_type=F32)
        vals = jnp.dot(rows_v[...], wv[:, cols], preferred_element_type=F32)
        for h in range(g, min(g + 4, nh)):
            cut = slice((h - g) * HD, (h - g + 1) * HD)
            kv[h, band] = jnp.concatenate([keys[:, cut], vals[:, cut]], axis=1).astype(BF16)
    for h in range(nh):
        if h < 2:
            for d in range(1, n_chips):
                kv_direct(h, d).start()
        kv_own(h).start()

    loads[5].wait()
    queries = jnp.dot(tok[...].reshape(n_rows, -1), wq[...], preferred_element_type=F32) * SCALE
    for h in range(nh):
        two = queries[:, (h // 2) * BLK : (h // 2 + 1) * BLK]
        if h % 2:
            two = pltpu.roll(two, HD, 1)
        q_pad[h] = jnp.where(low_half, two, 0.0).astype(BF16)

    tq = n_rows // 2

    def span(b):
        return pl.ds(pl.multiple_of(b * W, W), W)

    def score(h, b, i):
        r = slice(i * tq, (i + 1) * tq)
        q = jnp.concatenate([q_pad[h, r, :], bias[r, :]], axis=1)
        k = jnp.concatenate([kv[h, b], onehot[span(b), :]], axis=1)
        return lax.dot_general(q, k, NT, preferred_element_type=F32)

    def gather(s, h, b, i, first):
        r = slice(i * tq, (i + 1) * tq)
        cut = [s[:, j * BLK : (j + 1) * BLK] for j in range(KEEP)]
        m = jnp.broadcast_to(functools.reduce(jnp.maximum, cut).max(axis=1, keepdims=True), (tq, BLK))
        if not first:
            before = top[h, r, :]
            m = jnp.maximum(before, m)
        top[h, r, :] = m
        p = jnp.concatenate([jnp.exp2((x - m).astype(BF16)) for x in cut], axis=1)
        tile_kv = kv[h, b]
        v = jnp.where(low_half, jnp.ones_like(tile_kv), tile_kv)
        a = jnp.dot(p, v, preferred_element_type=F32)
        if not first:
            a = a + acc[h, r, :] * jnp.exp2(before - m)
        acc[h, r, :] = a

    def block(h, bands, first):
        units = [(b, i, first and n == 0) for n, b in enumerate(bands) for i in range(2)]
        s = score(h, *units[0][:2])
        for n, (b, i, start) in enumerate(units):
            after = score(h, *units[n + 1][:2]) if n + 1 < len(units) else None
            gather(s, h, b, i, start)
            s = after

    def local_block(h, _):
        @pl.when((h >= 1) & (h + 1 < nh))
        def _():
            for d in range(1, n_chips):
                kv_direct(h + 1, d).start()

        @pl.when(h == nh // 2)
        def _():
            for d in range(1, n_chips):
                kv_arrived(0, chip_at(d) * 2 + core)
                kv_forward(0, d).start()

        kv_arrived(h, sibling)
        block(h, (band, sibling), True)
        return 0

    lax.fori_loop(0, nh, local_block, 0)

    for d in range(1, nz):
        w_arrived(d, my_part)
        for t in range(nt):
            (w_second(d, t) if t else w_third(d, 0)).start()

    def a_copy(h, d):
        to = lax.rem(z + d, nz)
        return remote(att.at[h, to], got.at[h, z], a_send.at[h, d], a_recv.at[h, z], {"head": to})

    def a_arrived(h, d):
        origin = lax.rem(z + d, nz)
        remote(att.at[h, origin], got.at[h, origin], a_send.at[h, d], a_recv.at[h, origin], {"head": origin}).wait_recv()

    def far_block(h, _):
        @pl.when(h + 1 < nh)
        def _():
            for d in range(1, n_chips):
                kv_arrived(h + 1, chip_at(d) * 2 + core)
                kv_forward(h + 1, d).start()

        @pl.when(h == nh - 1)
        def _():
            for t in range(1, nt):
                for d in range(1, nz):
                    w_arrived(d, lax.rem(tile + t, nt) * 2 + core)
                    w_third(d, t).start()

        for d in range(1, n_chips):
            other = chip_at(d) * 2
            kv_arrived(h, other + 1 - core)
            block(h, (other + core, other + 1 - core), False)
        for p in range(nz):
            a0 = acc[h, p * 2 * half : p * 2 * half + half, :]
            a1 = acc[h, p * 2 * half + half : (p + 1) * 2 * half, :]
            value = jnp.where(low_half, pltpu.roll(a0, HD, 1), a1)
            mass = jnp.where(low_half, a0, pltpu.roll(a1, HD, 1))
            att[h, p] = (value / mass).astype(BF16)
        for d in range(1, nz):
            a_copy(h, d).start()
        got[h, z] = att[h, z]
        return 0

    lax.fori_loop(0, nh, far_block, 0)

    for t in range(nt):
        for d in range(1, nz):
            w_arrived(d, lax.rem(tile + t, nt) * 2 + 1 - core)
    loads[6].wait()

    def heads(hs):
        return jnp.concatenate(
            [
                jnp.concatenate([got[h, s][:, r * HD : (r + 1) * HD] for s in range(nz) for h in hs], axis=1)
                for r in range(2)
            ],
            axis=0,
        )

    def weights(hs):
        return jnp.concatenate([wo[s, hs[0] * HD : (hs[-1] + 1) * HD, :] for s in range(nz)], axis=0)

    early, last = list(range(nh - 1)), [nh - 1]
    for h in early:
        for d in range(1, nz):
            a_arrived(h, d)
    pre[...] = jnp.dot(heads(early), weights(early), preferred_element_type=F32)
    for d in range(1, nz):
        a_arrived(nh - 1, d)
    out[...] = (pre[...] + jnp.dot(heads(last), weights(last), preferred_element_type=F32)).astype(BF16)

    for h in range(nh):
        kv_own(h).wait_send()
        for d in range(1, n_chips):
            kv_direct(h, d).wait_send()
            kv_forward(h, d).wait_send()
        for d in range(1, nz):
            a_copy(h, d).wait_send()
    for d in range(1, nz):
        w_first(d).wait_send()
        for t in range(nt):
            w_third(d, t).wait_send()
            if t:
                w_second(d, t).wait_send()


def on_device(nt, nb, nz, tokens, w_query, w_key, w_value, w_out, block_mask):
    nh = w_query.shape[1] // HD
    n_rows, width = tokens.shape
    nq = n_rows // BLK
    out_rows = n_rows // nz
    slots = -(-nb * KEEP // 128) * 128
    hbm = pl.BlockSpec(memory_space=pl.ANY)
    vmem = pltpu.VMEM
    dma = pltpu.SemaphoreType.DMA
    return pl.pallas_call(
        functools.partial(layer, nt, nb, nz),
        out_shape=jax.ShapeDtypeStruct((out_rows, w_out.shape[1]), BF16),
        in_specs=[hbm] * 6,
        out_specs=pl.BlockSpec(memory_space=pltpu.VMEM),
        scratch_shapes=[
            pltpu.SMEM(block_mask.shape, I32),
            vmem(block_mask.shape, I32),
            vmem((nq, BLK, width), BF16),
            vmem(w_query.shape, BF16),
            vmem(w_key.shape, BF16),
            vmem(w_value.shape, BF16),
            vmem((W, width), BF16),
            vmem((nh, nb, W, 2 * HD), BF16),
            vmem((nh, n_rows, 2 * HD), BF16),
            vmem((n_rows, slots), BF16),
            vmem((nb * W, slots), BF16),
            vmem((nh, n_rows, 128), F32),
            vmem((nh, n_rows, 128), F32),
            vmem((nh, nz, out_rows // 2, 2 * HD), BF16),
            vmem((nh, nz, out_rows // 2, 2 * HD), BF16),
            vmem((nz,) + w_out.shape, BF16),
            vmem((out_rows, w_out.shape[1]), F32),
            dma((7,)),
            dma((nh, nb // 2)),
            dma((nh, nb // 2)),
            dma((nh, nb)),
            dma((nh, nz)),
            dma((nh, nz)),
            dma((nz,)),
            dma((nz, nt)),
            dma((nz, nt)),
            dma((nz, 2 * nt)),
        ],
        compiler_params=pltpu.CompilerParams(
            collective_id=0, has_side_effects=True, vmem_limit_bytes=58 * MIB
        ),
        name="layer",
    )(block_mask, tokens.reshape(nq, BLK, width), w_query, w_key, w_value, w_out)


def solution(mesh):
    return jax.shard_map(
        functools.partial(on_device, mesh.shape["tiles"], mesh.shape["band"], mesh.shape["head"]),
        mesh=mesh,
        in_specs=(
            P(("tiles", "band"), None),
            P(None, "head"),
            P(None, "head"),
            P(None, "head"),
            P("head", None),
            P("tiles", None),
        ),
        out_specs=P(("tiles", "band", "head"), None),
        check_vma=False,
    )
```

```python
import functools
import jax
import jax.numpy as jnp
from jax import lax
from jax.experimental import pallas as pl
from jax.experimental.pallas import tpu as pltpu
from jax.sharding import PartitionSpec as P

HD = 64
BLK = 128
KEEP = 6
LOW = -float(2**100)
SCALE = HD**-0.5 * 1.4426950408889634
MIB = 1 << 20
BF16 = jnp.bfloat16
F32 = jnp.float32
I32 = jnp.int32
NT = (((1,), (1,)), ((), ()))
W = KEEP * BLK


def select_blocks(mask, me, per_band):
    named = []
    for i in range(per_band):
        named.append(
            functools.reduce(jnp.maximum, [mask[r, me * per_band + i] for r in range(mask.shape[0])])
        )
    picks, rank = [0] * KEEP, 0
    for i in range(per_band):
        for k in range(min(i + 1, KEEP)):
            picks[k] = picks[k] + i * named[i] * (rank == k)
        rank = rank + named[i]
    return picks


def make_bias(mask, me, nb, bias):
    n_rows, n_kb = mask.shape
    nq = n_kb // nb
    slots = bias.shape[1]
    everything = mask[...].astype(F32).T
    rows = mask[pl.ds(pl.multiple_of(me * nq, nq), nq), :].astype(F32)
    named = jnp.broadcast_to(jnp.max(everything, axis=1, keepdims=True), (n_kb, slots))
    left = lax.broadcasted_iota(I32, (n_kb, n_kb), 0)
    right = lax.broadcasted_iota(I32, (n_kb, n_kb), 1)
    earlier = ((right < left) & (left // nq == right // nq)).astype(F32)
    rank = jnp.dot(earlier, named, preferred_element_type=F32)
    band = (lax.broadcasted_iota(I32, (n_kb, slots), 0) // nq).astype(F32)
    slot = lax.broadcasted_iota(I32, (n_kb, slots), 1).astype(F32)
    place = jnp.where((slot == band * KEEP + rank) & (named > 0) & (rank < KEEP), 1.0, 0.0)
    allowed = jnp.dot(rows, place, preferred_element_type=F32)
    value = jnp.where(allowed > 0, 0.0, LOW)
    for i in range(nq):
        bias[i * BLK : (i + 1) * BLK, :] = jnp.broadcast_to(value[i : i + 1, :], (BLK, slots)).astype(BF16)


def layer(
    nt, nb, nz, mask_h, tok_h, wq_h, wk_h, wv_h, wo_h, out,
    mask_s, mask_v, tok, wq, wk, wv, made, kv, q_pad, bias, onehot, top, acc, att, got, wo, pre,
    load, kv_send, kv_fwd, kv_recv, a_send, a_recv, w1_send, w2_send, w3_send, w_recv,
):
    nh = q_pad.shape[0]
    nq = tok.shape[0]
    n_chips = nb // 2
    slots = bias.shape[1]
    n_rows = nq * BLK
    depth = wo.shape[1]
    parts = 2 * nt
    per_part = depth // parts
    half = att.shape[2]
    tile, band, z = lax.axis_index("tiles"), lax.axis_index("band"), lax.axis_index("head")
    chip, core = band // 2, lax.rem(band, 2)
    sibling = chip * 2 + 1 - core
    mesh_id = pl.DeviceIdType.MESH

    pairs = ((mask_h, mask_s), (mask_h, mask_v), (tok_h, tok), (wk_h, wk), (wv_h, wv), (wq_h, wq), (wo_h, wo.at[z]))
    loads = [pltpu.make_async_copy(a, b, load.at[i]) for i, (a, b) in enumerate(pairs)]
    for c in loads:
        c.start()

    def chip_at(step):
        return lax.rem(chip + step, n_chips)

    peers = [{"band": sibling}]
    peers += [{"band": chip_at(d) * 2 + core} for d in range(1, n_chips)]
    peers += [{"head": lax.rem(z + d, nz)} for d in range(1, nz)]
    peers += [{"tiles": lax.rem(tile + d, nt)} for d in range(1, nt)]
    barrier = pltpu.get_barrier_semaphore()
    for p in peers:
        pl.semaphore_signal(barrier, inc=1, device_id=p, device_id_type=mesh_id)

    def remote(src, dst, send, recv, to):
        return pltpu.make_async_remote_copy(
            src_ref=src, dst_ref=dst, send_sem=send, recv_sem=recv, device_id=to, device_id_type=mesh_id
        )

    def kv_copy(h, origin, send, to):
        return remote(kv.at[h, origin], kv.at[h, origin], send, kv_recv.at[h, origin], {"band": to})

    def kv_direct(h, step):
        return kv_copy(h, band, kv_send.at[h, step], chip_at(step) * 2 + core)

    def kv_own(h):
        return kv_copy(h, band, kv_send.at[h, 0], sibling)

    def kv_forward(h, step):
        return kv_copy(h, chip_at(step) * 2 + core, kv_fwd.at[h, step], sibling)

    def kv_arrived(h, origin):
        kv_copy(h, origin, kv_recv.at[h, origin], sibling).wait_recv()

    def w_piece(source, part):
        return wo.at[source, pl.ds(pl.multiple_of(part * per_part, per_part), per_part)]

    my_part = tile * 2 + core

    def w_first(d):
        here = pl.ds(pl.multiple_of(my_part * per_part, per_part), per_part)
        return remote(
            wo_h.at[here], w_piece(z, my_part), w1_send.at[d], w_recv.at[z, my_part], {"head": lax.rem(z + d, nz)}
        )

    def w_second(d, t):
        source = lax.rem(z + d, nz)
        piece = w_piece(source, my_part)
        return remote(piece, piece, w2_send.at[d, t], w_recv.at[source, my_part], {"tiles": lax.rem(tile + t, nt)})

    def w_third(d, t):
        source, part = lax.rem(z + d, nz), lax.rem(tile + t, nt) * 2 + core
        piece = w_piece(source, part)
        return remote(piece, piece, w3_send.at[d, t], w_recv.at[source, part], {"band": sibling})

    def w_arrived(d, part):
        source = lax.rem(z + d, nz)
        piece = w_piece(source, part)
        remote(piece, piece, w1_send.at[d], w_recv.at[source, part], {"band": sibling}).wait_recv()

    slot_of = lax.broadcasted_iota(I32, (BLK, slots), 1)
    for s in range(nb * KEEP):
        onehot[s * BLK : (s + 1) * BLK, :] = jnp.where(slot_of == s, 1.0, 0.0).astype(BF16)
    loads[0].wait()
    sel = select_blocks(mask_s, band, nq)
    pl.semaphore_wait(barrier, len(peers))
    for d in range(1, nz):
        w_first(d).start()

    lane = lax.broadcasted_iota(I32, (1, BLK), 1)
    low_half = lane < HD

    for c in loads[2:5]:
        c.wait()
    for g in range(0, nh, 2):
        cols = slice(g * HD, (g + 2) * HD)
        both = jnp.dot(
            tok[...].reshape(n_rows, -1), jnp.concatenate([wk[:, cols], wv[:, cols]], axis=1),
            preferred_element_type=F32,
        )
        keys, vals = both[:, :BLK], both[:, BLK:]
        made[0] = jnp.where(low_half, keys, pltpu.roll(vals, HD, 1)).astype(BF16).reshape(nq, BLK, BLK)
        made[1] = jnp.where(low_half, pltpu.roll(keys, HD, 1), vals).astype(BF16).reshape(nq, BLK, BLK)
        for h in range(2):
            for k in range(KEEP):
                kv[g + h, band, k * BLK : (k + 1) * BLK, :] = made[h, sel[k]]
        for h in (g, g + 1):
            if h < 2:
                for d in range(1, n_chips):
                    kv_direct(h, d).start()
            kv_own(h).start()

    loads[5].wait()
    queries = jnp.dot(tok[...].reshape(n_rows, -1), wq[...], preferred_element_type=F32) * SCALE
    for h in range(nh):
        two = queries[:, (h // 2) * BLK : (h // 2 + 1) * BLK]
        if h % 2:
            two = pltpu.roll(two, HD, 1)
        q_pad[h] = jnp.where(low_half, two, 0.0).astype(BF16)

    loads[1].wait()
    make_bias(mask_v, band, nb, bias)
    tq = n_rows // 2

    def span(b):
        return pl.ds(pl.multiple_of(b * W, W), W)

    def score(h, b, i):
        r = slice(i * tq, (i + 1) * tq)
        q = jnp.concatenate([q_pad[h, r, :], bias[r, :]], axis=1)
        k = jnp.concatenate([kv[h, b], onehot[span(b), :]], axis=1)
        return lax.dot_general(q, k, NT, preferred_element_type=F32)

    def gather(s, h, b, i, first):
        r = slice(i * tq, (i + 1) * tq)
        cut = [s[:, j * BLK : (j + 1) * BLK] for j in range(KEEP)]
        m = jnp.broadcast_to(functools.reduce(jnp.maximum, cut).max(axis=1, keepdims=True), (tq, BLK))
        if not first:
            before = top[h, r, :]
            m = jnp.maximum(before, m)
        top[h, r, :] = m
        p = jnp.concatenate([jnp.exp2((x - m).astype(BF16)) for x in cut], axis=1)
        tile_kv = kv[h, b]
        v = jnp.where(low_half, jnp.ones_like(tile_kv), tile_kv)
        a = jnp.dot(p, v, preferred_element_type=F32)
        if not first:
            a = a + acc[h, r, :] * jnp.exp2(before - m)
        acc[h, r, :] = a

    def block(h, bands, first):
        units = [(b, i, first and n == 0) for n, b in enumerate(bands) for i in range(2)]
        s = score(h, *units[0][:2])
        for n, (b, i, start) in enumerate(units):
            after = score(h, *units[n + 1][:2]) if n + 1 < len(units) else None
            gather(s, h, b, i, start)
            s = after

    def local_block(h, _):
        @pl.when((h >= 1) & (h + 1 < nh))
        def _():
            for d in range(1, n_chips):
                kv_direct(h + 1, d).start()

        kv_arrived(h, sibling)
        block(h, (band, sibling), True)
        return 0

    lax.fori_loop(0, nh, local_block, 0)

    def a_copy(h, d):
        to = lax.rem(z + d, nz)
        return remote(att.at[h, to], got.at[h, z], a_send.at[h, d], a_recv.at[h, z], {"head": to})

    def a_arrived(h, d):
        origin = lax.rem(z + d, nz)
        remote(att.at[h, origin], got.at[h, origin], a_send.at[h, d], a_recv.at[h, origin], {"head": origin}).wait_recv()

    def far_block(h, _):
        @pl.when(h == 1)
        def _():
            for d in range(1, nz):
                w_arrived(d, my_part)
                for t in range(nt):
                    (w_second(d, t) if t else w_third(d, 0)).start()

        for d in range(1, n_chips):
            same = chip_at(d) * 2 + core
            kv_arrived(h, same)
            kv_forward(h, d).start()
            block(h, (same,), False)
            kv_arrived(h, chip_at(d) * 2 + 1 - core)
            block(h, (chip_at(d) * 2 + 1 - core,), False)
        for p in range(nz):
            a0 = acc[h, p * 2 * half : p * 2 * half + half, :]
            a1 = acc[h, p * 2 * half + half : (p + 1) * 2 * half, :]
            value = jnp.where(low_half, pltpu.roll(a0, HD, 1), a1)
            mass = jnp.where(low_half, a0, pltpu.roll(a1, HD, 1))
            att[h, p] = (value / mass).astype(BF16)
        for d in range(1, nz):
            a_copy(h, d).start()
        got[h, z] = att[h, z]
        return 0

    lax.fori_loop(0, nh, far_block, 0)

    for t in range(1, nt):
        for d in range(1, nz):
            w_arrived(d, lax.rem(tile + t, nt) * 2 + core)
            w_third(d, t).start()
    for t in range(nt):
        for d in range(1, nz):
            w_arrived(d, lax.rem(tile + t, nt) * 2 + 1 - core)
    loads[6].wait()

    def heads(hs):
        return jnp.concatenate(
            [
                jnp.concatenate([got[h, s][:, r * HD : (r + 1) * HD] for s in range(nz) for h in hs], axis=1)
                for r in range(2)
            ],
            axis=0,
        )

    def weights(hs):
        return jnp.concatenate([wo[s, hs[0] * HD : (hs[-1] + 1) * HD, :] for s in range(nz)], axis=0)

    early, last = list(range(nh - 1)), [nh - 1]
    for h in early:
        for d in range(1, nz):
            a_arrived(h, d)
    pre[...] = jnp.dot(heads(early), weights(early), preferred_element_type=F32)
    for d in range(1, nz):
        a_arrived(nh - 1, d)
    out[...] = (pre[...] + jnp.dot(heads(last), weights(last), preferred_element_type=F32)).astype(BF16)

    for h in range(nh):
        kv_own(h).wait_send()
        for d in range(1, n_chips):
            kv_direct(h, d).wait_send()
            kv_forward(h, d).wait_send()
        for d in range(1, nz):
            a_copy(h, d).wait_send()
    for d in range(1, nz):
        w_first(d).wait_send()
        for t in range(nt):
            w_third(d, t).wait_send()
            if t:
                w_second(d, t).wait_send()


def on_device(nt, nb, nz, tokens, w_query, w_key, w_value, w_out, block_mask):
    nh = w_query.shape[1] // HD
    n_rows, width = tokens.shape
    nq = n_rows // BLK
    out_rows = n_rows // nz
    slots = -(-nb * KEEP // 128) * 128
    hbm = pl.BlockSpec(memory_space=pltpu.HBM)
    vmem = pltpu.VMEM
    dma = pltpu.SemaphoreType.DMA
    return pl.pallas_call(
        functools.partial(layer, nt, nb, nz),
        out_shape=jax.ShapeDtypeStruct((out_rows, w_out.shape[1]), BF16),
        in_specs=[hbm] * 6,
        out_specs=pl.BlockSpec(memory_space=pltpu.VMEM),
        scratch_shapes=[
            pltpu.SMEM(block_mask.shape, I32),
            vmem(block_mask.shape, I32),
            vmem((nq, BLK, width), BF16),
            vmem(w_query.shape, BF16),
            vmem(w_key.shape, BF16),
            vmem(w_value.shape, BF16),
            vmem((2, nq, BLK, 2 * HD), BF16),
            vmem((nh, nb, W, 2 * HD), BF16),
            vmem((nh, n_rows, 2 * HD), BF16),
            vmem((n_rows, slots), BF16),
            vmem((nb * W, slots), BF16),
            vmem((nh, n_rows, 128), F32),
            vmem((nh, n_rows, 128), F32),
            vmem((nh, nz, out_rows // 2, 2 * HD), BF16),
            vmem((nh, nz, out_rows // 2, 2 * HD), BF16),
            vmem((nz,) + w_out.shape, BF16),
            vmem((out_rows, w_out.shape[1]), F32),
            dma((7,)),
            dma((nh, nb // 2)),
            dma((nh, nb // 2)),
            dma((nh, nb)),
            dma((nh, nz)),
            dma((nh, nz)),
            dma((nz,)),
            dma((nz, nt)),
            dma((nz, nt)),
            dma((nz, 2 * nt)),
        ],
        compiler_params=pltpu.CompilerParams(
            collective_id=0, has_side_effects=True, vmem_limit_bytes=53 * MIB
        ),
        name="layer",
    )(block_mask, tokens.reshape(nq, BLK, width), w_query, w_key, w_value, w_out)


def solution(mesh):
    return jax.shard_map(
        functools.partial(on_device, mesh.shape["tiles"], mesh.shape["band"], mesh.shape["head"]),
        mesh=mesh,
        in_specs=(
            P(("tiles", "band"), None),
            P(None, "head"),
            P(None, "head"),
            P(None, "head"),
            P("head", None),
            P("tiles", None),
        ),
        out_specs=P(("tiles", "band", "head"), None),
        check_vma=False,
    )
```

```python
import functools
import jax
import jax.numpy as jnp
from jax import lax
from jax.experimental import pallas as pl
from jax.experimental.pallas import tpu as pltpu
from jax.sharding import PartitionSpec as P

HD = 64
BLK = 128
KEEP = 6
LOW = -float(2**100)
SCALE = HD**-0.5 * 1.4426950408889634
MIB = 1 << 20
BF16 = jnp.bfloat16
F32 = jnp.float32
I32 = jnp.int32
NT = (((1,), (1,)), ((), ()))
W = KEEP * BLK


def select_blocks(mask, me, per_band):
    named = []
    for i in range(per_band):
        named.append(
            functools.reduce(jnp.maximum, [mask[r, me * per_band + i] for r in range(mask.shape[0])])
        )
    picks, rank = [0] * KEEP, 0
    for i in range(per_band):
        for k in range(min(i + 1, KEEP)):
            picks[k] = picks[k] + i * named[i] * (rank == k)
        rank = rank + named[i]
    return picks


def make_bias(mask, me, nb, bias):
    n_rows, n_kb = mask.shape
    nq = n_kb // nb
    slots = bias.shape[1]
    everything = mask[...].astype(F32).T
    rows = mask[pl.ds(pl.multiple_of(me * nq, nq), nq), :].astype(F32)
    named = jnp.broadcast_to(jnp.max(everything, axis=1, keepdims=True), (n_kb, slots))
    left = lax.broadcasted_iota(I32, (n_kb, n_kb), 0)
    right = lax.broadcasted_iota(I32, (n_kb, n_kb), 1)
    earlier = ((right < left) & (left // nq == right // nq)).astype(F32)
    rank = jnp.dot(earlier, named, preferred_element_type=F32)
    band = (lax.broadcasted_iota(I32, (n_kb, slots), 0) // nq).astype(F32)
    slot = lax.broadcasted_iota(I32, (n_kb, slots), 1).astype(F32)
    place = jnp.where((slot == band * KEEP + rank) & (named > 0) & (rank < KEEP), 1.0, 0.0)
    allowed = jnp.dot(rows, place, preferred_element_type=F32)
    value = jnp.where(allowed > 0, 0.0, LOW)
    for i in range(nq):
        bias[i * BLK : (i + 1) * BLK, :] = jnp.broadcast_to(value[i : i + 1, :], (BLK, slots)).astype(BF16)


def layer(
    nt, nb, nz, mask_h, tok_h, wq_h, wk_h, wv_h, wo_h, out,
    mask_s, mask_v, tok, wq, wk, wv, made, kv, q_pad, bias, onehot, top, acc, att, got, wo, pre,
    load, kv_send, kv_fwd, kv_recv, a_send, a_recv, w1_send, w2_send, w3_send, w_recv,
):
    nh = q_pad.shape[0]
    nq = tok.shape[0]
    n_chips = nb // 2
    slots = bias.shape[1]
    n_rows = nq * BLK
    depth = wo.shape[1]
    parts = 2 * nt
    per_part = depth // parts
    half = att.shape[2]
    tile, band, z = lax.axis_index("tiles"), lax.axis_index("band"), lax.axis_index("head")
    chip, core = band // 2, lax.rem(band, 2)
    sibling = chip * 2 + 1 - core
    mesh_id = pl.DeviceIdType.MESH

    pairs = ((mask_h, mask_s), (mask_h, mask_v), (wk_h, wk), (wv_h, wv),
             (tok_h.at[: nq // 2], tok.at[: nq // 2]), (tok_h.at[nq // 2 :], tok.at[nq // 2 :]),
             (wq_h, wq), (wo_h, wo.at[z]))
    loads = [pltpu.make_async_copy(a, b, load.at[i]) for i, (a, b) in enumerate(pairs)]
    for c in loads:
        c.start()

    def chip_at(step):
        return lax.rem(chip + step, n_chips)

    peers = [{"band": sibling}]
    peers += [{"band": chip_at(d) * 2 + core} for d in range(1, n_chips)]
    peers += [{"head": lax.rem(z + d, nz)} for d in range(1, nz)]
    peers += [{"tiles": lax.rem(tile + d, nt)} for d in range(1, nt)]
    barrier = pltpu.get_barrier_semaphore()
    for p in peers:
        pl.semaphore_signal(barrier, inc=1, device_id=p, device_id_type=mesh_id)

    def remote(src, dst, send, recv, to):
        return pltpu.make_async_remote_copy(
            src_ref=src, dst_ref=dst, send_sem=send, recv_sem=recv, device_id=to, device_id_type=mesh_id
        )

    def kv_copy(h, origin, send, to):
        return remote(kv.at[h, origin], kv.at[h, origin], send, kv_recv.at[h, origin], {"band": to})

    def kv_direct(h, step):
        return kv_copy(h, band, kv_send.at[h, step], chip_at(step) * 2 + core)

    def kv_own(h):
        return kv_copy(h, band, kv_send.at[h, 0], sibling)

    def kv_forward(h, step):
        return kv_copy(h, chip_at(step) * 2 + core, kv_fwd.at[h, step], sibling)

    def kv_arrived(h, origin):
        kv_copy(h, origin, kv_recv.at[h, origin], sibling).wait_recv()

    def w_piece(source, part):
        return wo.at[source, pl.ds(pl.multiple_of(part * per_part, per_part), per_part)]

    my_part = tile * 2 + core

    def w_first(d):
        here = pl.ds(pl.multiple_of(my_part * per_part, per_part), per_part)
        return remote(
            wo_h.at[here], w_piece(z, my_part), w1_send.at[d], w_recv.at[z, my_part], {"head": lax.rem(z + d, nz)}
        )

    def w_second(d, t):
        source = lax.rem(z + d, nz)
        piece = w_piece(source, my_part)
        return remote(piece, piece, w2_send.at[d, t], w_recv.at[source, my_part], {"tiles": lax.rem(tile + t, nt)})

    def w_third(d, t):
        source, part = lax.rem(z + d, nz), lax.rem(tile + t, nt) * 2 + core
        piece = w_piece(source, part)
        return remote(piece, piece, w3_send.at[d, t], w_recv.at[source, part], {"band": sibling})

    def w_arrived(d, part):
        source = lax.rem(z + d, nz)
        piece = w_piece(source, part)
        remote(piece, piece, w1_send.at[d], w_recv.at[source, part], {"band": sibling}).wait_recv()

    slot_of = lax.broadcasted_iota(I32, (BLK, slots), 1)
    for s in range(nb * KEEP):
        onehot[s * BLK : (s + 1) * BLK, :] = jnp.where(slot_of == s, 1.0, 0.0).astype(BF16)
    loads[0].wait()
    sel = select_blocks(mask_s, band, nq)
    pl.semaphore_wait(barrier, len(peers))
    for d in range(1, nz):
        w_first(d).start()

    lane = lax.broadcasted_iota(I32, (1, BLK), 1)
    low_half = lane < HD

    loads[2].wait()
    loads[3].wait()
    for g in range(0, nh, 2):
        cols = slice(g * HD, (g + 2) * HD)
        weight = jnp.concatenate([wk[:, cols], wv[:, cols]], axis=1)
        for i in range(2):
            blocks = slice(i * nq // 2, (i + 1) * nq // 2)
            if g == 0:
                loads[4 + i].wait()
            both = jnp.dot(tok[blocks].reshape(n_rows // 2, -1), weight, preferred_element_type=F32)
            keys, vals = both[:, :BLK], both[:, BLK:]
            one = jnp.where(low_half, keys, pltpu.roll(vals, HD, 1)).astype(BF16)
            two = jnp.where(low_half, pltpu.roll(keys, HD, 1), vals).astype(BF16)
            made[0, blocks] = one.reshape(nq // 2, BLK, BLK)
            made[1, blocks] = two.reshape(nq // 2, BLK, BLK)
        for h in range(2):
            for k in range(KEEP):
                kv[g + h, band, k * BLK : (k + 1) * BLK, :] = made[h, sel[k]]
        for h in (g, g + 1):
            if h < 2:
                for d in range(1, n_chips):
                    kv_direct(h, d).start()
            kv_own(h).start()

    loads[6].wait()
    queries = jnp.dot(tok[...].reshape(n_rows, -1), wq[...], preferred_element_type=F32) * SCALE
    for h in range(nh):
        two = queries[:, (h // 2) * BLK : (h // 2 + 1) * BLK]
        if h % 2:
            two = pltpu.roll(two, HD, 1)
        q_pad[h] = jnp.where(low_half, two, 0.0).astype(BF16)

    loads[1].wait()
    make_bias(mask_v, band, nb, bias)
    tq = n_rows // 2
    far = (z * 2) // nz

    def part(i):
        return pl.ds(pl.multiple_of(lax.rem(i + 1 + far, 2) * tq, tq), tq)

    def span(b):
        return pl.ds(pl.multiple_of(b * W, W), W)

    def score(h, b, i):
        r = part(i)
        q = jnp.concatenate([q_pad[h, r, :], bias[r, :]], axis=1)
        k = jnp.concatenate([kv[h, b], onehot[span(b), :]], axis=1)
        return lax.dot_general(q, k, NT, preferred_element_type=F32)

    def gather(s, h, b, i, first):
        r = part(i)
        cut = [s[:, j * BLK : (j + 1) * BLK] for j in range(KEEP)]
        m = jnp.broadcast_to(functools.reduce(jnp.maximum, cut).max(axis=1, keepdims=True), (tq, BLK))
        if not first:
            before = top[h, r, :]
            m = jnp.maximum(before, m)
        top[h, r, :] = m
        p = jnp.concatenate([jnp.exp2((x - m).astype(BF16)) for x in cut], axis=1)
        tile_kv = kv[h, b]
        v = jnp.where(low_half, jnp.ones_like(tile_kv), tile_kv)
        a = jnp.dot(p, v, preferred_element_type=F32)
        if not first:
            a = a + acc[h, r, :] * jnp.exp2(before - m)
        acc[h, r, :] = a

    def block(h, bands, first, done=None):
        units = [(b, i, first and n == 0) for n, b in enumerate(bands) for i in range(2)]
        s = score(h, *units[0][:2])
        for n, (b, i, start) in enumerate(units):
            after = score(h, *units[n + 1][:2]) if n + 1 < len(units) else None
            gather(s, h, b, i, start)
            if done is not None:
                done(i)
            s = after

    def local_block(h, _):
        @pl.when((h >= 1) & (h + 1 < nh))
        def _():
            for d in range(1, n_chips):
                kv_direct(h + 1, d).start()

        kv_arrived(h, sibling)
        block(h, (band, sibling), True)
        return 0

    lax.fori_loop(0, nh, local_block, 0)

    def a_copy(h, d):
        to = lax.rem(z + d, nz)
        return remote(att.at[h, to], got.at[h, z], a_send.at[h, d], a_recv.at[h, z], {"head": to})

    def a_arrived(h, d):
        origin = lax.rem(z + d, nz)
        remote(att.at[h, origin], got.at[h, origin], a_send.at[h, d], a_recv.at[h, origin], {"head": origin}).wait_recv()

    reach = nz // 2

    def finish(h, i):
        base = lax.rem(far + 1 + i, 2) * reach
        order = [lax.rem(z + e, reach) + base for e in range(reach)]
        for p in order:
            lo = p * 2 * half
            a0 = acc[h, pl.ds(pl.multiple_of(lo, half), half), :]
            a1 = acc[h, pl.ds(pl.multiple_of(lo + half, half), half), :]
            value = jnp.where(low_half, pltpu.roll(a0, HD, 1), a1)
            mass = jnp.where(low_half, a0, pltpu.roll(a1, HD, 1))
            att[h, p] = (value / mass).astype(BF16)

    def far_block(h, _):
        @pl.when(h == 1)
        def _():
            for d in range(1, nz):
                w_arrived(d, my_part)
                for t in range(nt):
                    (w_second(d, t) if t else w_third(d, 0)).start()

        for d in range(1, n_chips):
            same = chip_at(d) * 2 + core
            kv_arrived(h, same)
            kv_forward(h, d).start()
            block(h, (same,), False)
            kv_arrived(h, chip_at(d) * 2 + 1 - core)
            block(h, (chip_at(d) * 2 + 1 - core,), False, functools.partial(finish, h) if d == n_chips - 1 else None)
        for d in range(1, nz):
            a_copy(h, d).start()
        got[h, z] = att[h, z]
        return 0

    lax.fori_loop(0, nh, far_block, 0)

    for t in range(1, nt):
        for d in range(1, nz):
            w_arrived(d, lax.rem(tile + t, nt) * 2 + core)
            w_third(d, t).start()
    for t in range(nt):
        for d in range(1, nz):
            w_arrived(d, lax.rem(tile + t, nt) * 2 + 1 - core)
    loads[7].wait()

    def heads(hs):
        return jnp.concatenate(
            [
                jnp.concatenate([got[h, s][:, r * HD : (r + 1) * HD] for s in range(nz) for h in hs], axis=1)
                for r in range(2)
            ],
            axis=0,
        )

    def weights(hs):
        return jnp.concatenate([wo[s, hs[0] * HD : (hs[-1] + 1) * HD, :] for s in range(nz)], axis=0)

    early, last = list(range(nh - 1)), [nh - 1]
    for h in early:
        for d in range(1, nz):
            a_arrived(h, d)
    pre[...] = jnp.dot(heads(early), weights(early), preferred_element_type=F32)
    for d in range(1, nz):
        a_arrived(nh - 1, d)
    out[...] = (pre[...] + jnp.dot(heads(last), weights(last), preferred_element_type=F32)).astype(BF16)

    for h in range(nh):
        kv_own(h).wait_send()
        for d in range(1, n_chips):
            kv_direct(h, d).wait_send()
            kv_forward(h, d).wait_send()
        for d in range(1, nz):
            a_copy(h, d).wait_send()
    for d in range(1, nz):
        w_first(d).wait_send()
        for t in range(nt):
            w_third(d, t).wait_send()
            if t:
                w_second(d, t).wait_send()


def on_device(nt, nb, nz, tokens, w_query, w_key, w_value, w_out, block_mask):
    nh = w_query.shape[1] // HD
    n_rows, width = tokens.shape
    nq = n_rows // BLK
    out_rows = n_rows // nz
    slots = -(-nb * KEEP // 128) * 128
    hbm = pl.BlockSpec(memory_space=pltpu.HBM)
    vmem = pltpu.VMEM
    dma = pltpu.SemaphoreType.DMA
    return pl.pallas_call(
        functools.partial(layer, nt, nb, nz),
        out_shape=jax.ShapeDtypeStruct((out_rows, w_out.shape[1]), BF16),
        in_specs=[hbm] * 6,
        out_specs=pl.BlockSpec(memory_space=pltpu.VMEM),
        scratch_shapes=[
            pltpu.SMEM(block_mask.shape, I32),
            vmem(block_mask.shape, I32),
            vmem((nq, BLK, width), BF16),
            vmem(w_query.shape, BF16),
            vmem(w_key.shape, BF16),
            vmem(w_value.shape, BF16),
            vmem((2, nq, BLK, 2 * HD), BF16),
            vmem((nh, nb, W, 2 * HD), BF16),
            vmem((nh, n_rows, 2 * HD), BF16),
            vmem((n_rows, slots), BF16),
            vmem((nb * W, slots), BF16),
            vmem((nh, n_rows, 128), F32),
            vmem((nh, n_rows, 128), F32),
            vmem((nh, nz, out_rows // 2, 2 * HD), BF16),
            vmem((nh, nz, out_rows // 2, 2 * HD), BF16),
            vmem((nz,) + w_out.shape, BF16),
            vmem((out_rows, w_out.shape[1]), F32),
            dma((8,)),
            dma((nh, nb // 2)),
            dma((nh, nb // 2)),
            dma((nh, nb)),
            dma((nh, nz)),
            dma((nh, nz)),
            dma((nz,)),
            dma((nz, nt)),
            dma((nz, nt)),
            dma((nz, 2 * nt)),
        ],
        compiler_params=pltpu.CompilerParams(
            collective_id=0, has_side_effects=True, vmem_limit_bytes=53 * MIB
        ),
        name="layer",
    )(block_mask, tokens.reshape(nq, BLK, width), w_query, w_key, w_value, w_out)


def solution(mesh):
    return jax.shard_map(
        functools.partial(on_device, mesh.shape["tiles"], mesh.shape["band"], mesh.shape["head"]),
        mesh=mesh,
        in_specs=(
            P(("tiles", "band"), None),
            P(None, "head"),
            P(None, "head"),
            P(None, "head"),
            P("head", None),
            P("tiles", None),
        ),
        out_specs=P(("tiles", "band", "head"), None),
        check_vma=False,
    )
```

```python
import functools
import jax
import jax.numpy as jnp
from jax import lax
from jax.experimental import pallas as pl
from jax.experimental.pallas import tpu as pltpu
from jax.sharding import PartitionSpec as P

HD = 64
BLK = 128
KEEP = 6
LOW = -float(2**100)
SCALE = HD**-0.5 * 1.4426950408889634
MIB = 1 << 20
BF16 = jnp.bfloat16
F32 = jnp.float32
I32 = jnp.int32
NT = (((1,), (1,)), ((), ()))
W = KEEP * BLK


def select_blocks(mask, me, per_band):
    named = []
    for i in range(per_band):
        named.append(
            functools.reduce(jnp.maximum, [mask[r, me * per_band + i] for r in range(mask.shape[0])])
        )
    picks, rank = [0] * KEEP, 0
    for i in range(per_band):
        for k in range(min(i + 1, KEEP)):
            picks[k] = picks[k] + i * named[i] * (rank == k)
        rank = rank + named[i]
    return picks


def make_bias(mask, me, nb, bias):
    n_rows, n_kb = mask.shape
    nq = n_kb // nb
    slots = bias.shape[1]
    everything = mask[...].astype(F32).T
    rows = mask[pl.ds(pl.multiple_of(me * nq, nq), nq), :].astype(F32)
    named = jnp.broadcast_to(jnp.max(everything, axis=1, keepdims=True), (n_kb, slots))
    left = lax.broadcasted_iota(I32, (n_kb, n_kb), 0)
    right = lax.broadcasted_iota(I32, (n_kb, n_kb), 1)
    earlier = ((right < left) & (left // nq == right // nq)).astype(F32)
    rank = jnp.dot(earlier, named, preferred_element_type=F32)
    band = (lax.broadcasted_iota(I32, (n_kb, slots), 0) // nq).astype(F32)
    slot = lax.broadcasted_iota(I32, (n_kb, slots), 1).astype(F32)
    place = jnp.where((slot == band * KEEP + rank) & (named > 0) & (rank < KEEP), 1.0, 0.0)
    allowed = jnp.dot(rows, place, preferred_element_type=F32)
    value = jnp.where(allowed > 0, 0.0, LOW)
    for i in range(nq):
        bias[i * BLK : (i + 1) * BLK, :] = jnp.broadcast_to(value[i : i + 1, :], (BLK, slots)).astype(BF16)


def layer(
    nt, nb, nz, mask_h, tok_h, wq_h, wk_h, wv_h, wo_h, out,
    mask_s, mask_v, tok, wq, wk, wv, made, kv, q_pad, bias, onehot, top, acc, att, got, wo, pre,
    load, kv_send, kv_fwd, kv_recv, a_send, a_recv, w1_send, w2_send, w3_send, w_recv,
):
    nh = q_pad.shape[0]
    nq = tok.shape[0]
    n_chips = nb // 2
    slots = bias.shape[1]
    n_rows = nq * BLK
    depth = wo.shape[1]
    parts = 2 * nt
    per_part = depth // parts
    half = att.shape[2]
    tile, band, z = lax.axis_index("tiles"), lax.axis_index("band"), lax.axis_index("head")
    chip, core = band // 2, lax.rem(band, 2)
    sibling = chip * 2 + 1 - core
    mesh_id = pl.DeviceIdType.MESH

    pairs = ((mask_h, mask_s), (mask_h, mask_v), (wk_h, wk), (wv_h, wv),
             (tok_h.at[: nq // 2], tok.at[: nq // 2]), (tok_h.at[nq // 2 :], tok.at[nq // 2 :]),
             (wq_h, wq), (wo_h, wo.at[z]))
    loads = [pltpu.make_async_copy(a, b, load.at[i]) for i, (a, b) in enumerate(pairs)]
    for c in loads:
        c.start()

    def chip_at(step):
        return lax.rem(chip + step, n_chips)

    peers = [{"band": sibling}]
    peers += [{"band": chip_at(d) * 2 + core} for d in range(1, n_chips)]
    peers += [{"head": lax.rem(z + d, nz)} for d in range(1, nz)]
    peers += [{"tiles": lax.rem(tile + d, nt)} for d in range(1, nt)]
    barrier = pltpu.get_barrier_semaphore()
    for p in peers:
        pl.semaphore_signal(barrier, inc=1, device_id=p, device_id_type=mesh_id)

    def remote(src, dst, send, recv, to):
        return pltpu.make_async_remote_copy(
            src_ref=src, dst_ref=dst, send_sem=send, recv_sem=recv, device_id=to, device_id_type=mesh_id
        )

    def kv_copy(h, origin, send, to):
        return remote(kv.at[h, origin], kv.at[h, origin], send, kv_recv.at[h, origin], {"band": to})

    def kv_direct(h, step):
        return kv_copy(h, band, kv_send.at[h, step], chip_at(step) * 2 + core)

    def kv_own(h):
        return kv_copy(h, band, kv_send.at[h, 0], sibling)

    def kv_forward(h, step):
        return kv_copy(h, chip_at(step) * 2 + core, kv_fwd.at[h, step], sibling)

    def kv_arrived(h, origin):
        kv_copy(h, origin, kv_recv.at[h, origin], sibling).wait_recv()

    def w_piece(source, part):
        return wo.at[source, pl.ds(pl.multiple_of(part * per_part, per_part), per_part)]

    my_part = tile * 2 + core

    def w_first(d):
        here = pl.ds(pl.multiple_of(my_part * per_part, per_part), per_part)
        return remote(
            wo_h.at[here], w_piece(z, my_part), w1_send.at[d], w_recv.at[z, my_part], {"head": lax.rem(z + d, nz)}
        )

    def w_second(d, t):
        source = lax.rem(z + d, nz)
        piece = w_piece(source, my_part)
        return remote(piece, piece, w2_send.at[d, t], w_recv.at[source, my_part], {"tiles": lax.rem(tile + t, nt)})

    def w_third(d, t):
        source, part = lax.rem(z + d, nz), lax.rem(tile + t, nt) * 2 + core
        piece = w_piece(source, part)
        return remote(piece, piece, w3_send.at[d, t], w_recv.at[source, part], {"band": sibling})

    def w_arrived(d, part):
        source = lax.rem(z + d, nz)
        piece = w_piece(source, part)
        remote(piece, piece, w1_send.at[d], w_recv.at[source, part], {"band": sibling}).wait_recv()

    slot_of = lax.broadcasted_iota(I32, (BLK, slots), 1)
    for s in range(nb * KEEP):
        onehot[s * BLK : (s + 1) * BLK, :] = jnp.where(slot_of == s, 1.0, 0.0).astype(BF16)
    loads[0].wait()
    sel = select_blocks(mask_s, band, nq)
    pl.semaphore_wait(barrier, len(peers))
    for d in range(1, nz):
        w_first(d).start()

    lane = lax.broadcasted_iota(I32, (1, BLK), 1)
    low_half = lane < HD

    loads[2].wait()
    loads[3].wait()
    for g in range(0, nh, 2):
        cols = slice(g * HD, (g + 2) * HD)
        weight = jnp.concatenate([wk[:, cols], wv[:, cols]], axis=1)
        for i in range(2):
            blocks = slice(i * nq // 2, (i + 1) * nq // 2)
            if g == 0:
                loads[4 + i].wait()
            both = jnp.dot(tok[blocks].reshape(n_rows // 2, -1), weight, preferred_element_type=F32)
            keys, vals = both[:, :BLK], both[:, BLK:]
            one = jnp.where(low_half, keys, pltpu.roll(vals, HD, 1)).astype(BF16)
            two = jnp.where(low_half, pltpu.roll(keys, HD, 1), vals).astype(BF16)
            made[0, blocks] = one.reshape(nq // 2, BLK, BLK)
            made[1, blocks] = two.reshape(nq // 2, BLK, BLK)
        for h in range(2):
            for k in range(KEEP):
                kv[g + h, band, k * BLK : (k + 1) * BLK, :] = made[h, sel[k]]
        for h in (g, g + 1):
            if h < 2:
                for d in range(1, n_chips):
                    kv_direct(h, d).start()
            kv_own(h).start()

    loads[6].wait()
    queries = jnp.dot(tok[...].reshape(n_rows, -1), wq[...], preferred_element_type=F32) * SCALE
    for h in range(nh):
        two = queries[:, (h // 2) * BLK : (h // 2 + 1) * BLK]
        if h % 2:
            two = pltpu.roll(two, HD, 1)
        q_pad[h] = jnp.where(low_half, two, 0.0).astype(BF16)

    loads[1].wait()
    make_bias(mask_v, band, nb, bias)
    tq = n_rows // 2
    far = (z * 2) // nz

    def part(i):
        return pl.ds(pl.multiple_of(lax.rem(i + 1 + far, 2) * tq, tq), tq)

    def span(b):
        return pl.ds(pl.multiple_of(b * W, W), W)

    def score(h, b, i):
        r = part(i)
        q = jnp.concatenate([q_pad[h, r, :], bias[r, :]], axis=1)
        k = jnp.concatenate([kv[h, b], onehot[span(b), :]], axis=1)
        return lax.dot_general(q, k, NT, preferred_element_type=F32)

    def gather(s, h, b, i, first):
        r = part(i)
        cut = [s[:, j * BLK : (j + 1) * BLK] for j in range(KEEP)]
        m = jnp.broadcast_to(functools.reduce(jnp.maximum, cut).max(axis=1, keepdims=True), (tq, BLK))
        if not first:
            before = top[h, r, :]
            m = jnp.maximum(before, m)
        top[h, r, :] = m
        p = jnp.concatenate([jnp.exp2((x - m).astype(BF16)) for x in cut], axis=1)
        tile_kv = kv[h, b]
        v = jnp.where(low_half, jnp.ones_like(tile_kv), tile_kv)
        a = jnp.dot(p, v, preferred_element_type=F32)
        if not first:
            a = a + acc[h, r, :] * jnp.exp2(before - m)
        acc[h, r, :] = a

    def block(h, bands, first, done=None):
        units = [(b, i, first and n == 0) for n, b in enumerate(bands) for i in range(2)]
        s = score(h, *units[0][:2])
        for n, (b, i, start) in enumerate(units):
            after = score(h, *units[n + 1][:2]) if n + 1 < len(units) else None
            gather(s, h, b, i, start)
            if done is not None:
                done(i)
            s = after

    def local_block(h, _):
        @pl.when((h >= 1) & (h + 1 < nh))
        def _():
            for d in range(1, n_chips):
                kv_direct(h + 1, d).start()

        kv_arrived(h, sibling)
        block(h, (band, sibling), True)
        return 0

    def a_copy(h, d):
        to = lax.rem(z + d, nz)
        return remote(att.at[h, to], got.at[h, z], a_send.at[h, d], a_recv.at[h, z], {"head": to})

    def a_arrived(h, d):
        origin = lax.rem(z + d, nz)
        remote(att.at[h, origin], got.at[h, origin], a_send.at[h, d], a_recv.at[h, origin], {"head": origin}).wait_recv()

    reach = nz // 2

    def finish(h, i):
        base = lax.rem(far + 1 + i, 2) * reach
        order = [lax.rem(z + e, reach) + base for e in range(reach)]
        for p in order:
            lo = p * 2 * half
            a0 = acc[h, pl.ds(pl.multiple_of(lo, half), half), :]
            a1 = acc[h, pl.ds(pl.multiple_of(lo + half, half), half), :]
            value = jnp.where(low_half, pltpu.roll(a0, HD, 1), a1)
            mass = jnp.where(low_half, a0, pltpu.roll(a1, HD, 1))
            att[h, p] = (value / mass).astype(BF16)

    def far_block(h, _):
        @pl.when(h == 1)
        def _():
            for d in range(1, nz):
                w_arrived(d, my_part)
                for t in range(nt):
                    (w_second(d, t) if t else w_third(d, 0)).start()

        for d in range(1, n_chips):
            same = chip_at(d) * 2 + core
            kv_arrived(h, same)
            kv_forward(h, d).start()
            block(h, (same,), False)
            kv_arrived(h, chip_at(d) * 2 + 1 - core)
            block(h, (chip_at(d) * 2 + 1 - core,), False, functools.partial(finish, h) if d == n_chips - 1 else None)
        for d in range(1, nz):
            a_copy(h, d).start()
        got[h, z] = att[h, z]
        return 0

    def turn(i, _):
        @pl.when(i < nh)
        def _():
            local_block(i, 0)

        @pl.when(i >= 2)
        def _():
            far_block(i - 2, 0)

        return 0

    lax.fori_loop(0, nh + 2, turn, 0)

    for t in range(1, nt):
        for d in range(1, nz):
            w_arrived(d, lax.rem(tile + t, nt) * 2 + core)
            w_third(d, t).start()
    for t in range(nt):
        for d in range(1, nz):
            w_arrived(d, lax.rem(tile + t, nt) * 2 + 1 - core)
    loads[7].wait()

    def heads(hs):
        return jnp.concatenate(
            [
                jnp.concatenate([got[h, s][:, r * HD : (r + 1) * HD] for s in range(nz) for h in hs], axis=1)
                for r in range(2)
            ],
            axis=0,
        )

    def weights(hs):
        return jnp.concatenate([wo[s, hs[0] * HD : (hs[-1] + 1) * HD, :] for s in range(nz)], axis=0)

    early, last = list(range(nh - 1)), [nh - 1]
    for h in early:
        for d in range(1, nz):
            a_arrived(h, d)
    pre[...] = jnp.dot(heads(early), weights(early), preferred_element_type=F32)
    for d in range(1, nz):
        a_arrived(nh - 1, d)
    out[...] = (pre[...] + jnp.dot(heads(last), weights(last), preferred_element_type=F32)).astype(BF16)

    for h in range(nh):
        kv_own(h).wait_send()
        for d in range(1, n_chips):
            kv_direct(h, d).wait_send()
            kv_forward(h, d).wait_send()
        for d in range(1, nz):
            a_copy(h, d).wait_send()
    for d in range(1, nz):
        w_first(d).wait_send()
        for t in range(nt):
            w_third(d, t).wait_send()
            if t:
                w_second(d, t).wait_send()


def on_device(nt, nb, nz, tokens, w_query, w_key, w_value, w_out, block_mask):
    nh = w_query.shape[1] // HD
    n_rows, width = tokens.shape
    nq = n_rows // BLK
    out_rows = n_rows // nz
    slots = -(-nb * KEEP // 128) * 128
    hbm = pl.BlockSpec(memory_space=pltpu.HBM)
    vmem = pltpu.VMEM
    dma = pltpu.SemaphoreType.DMA
    return pl.pallas_call(
        functools.partial(layer, nt, nb, nz),
        out_shape=jax.ShapeDtypeStruct((out_rows, w_out.shape[1]), BF16),
        in_specs=[hbm] * 6,
        out_specs=pl.BlockSpec(memory_space=pltpu.VMEM),
        scratch_shapes=[
            pltpu.SMEM(block_mask.shape, I32),
            vmem(block_mask.shape, I32),
            vmem((nq, BLK, width), BF16),
            vmem(w_query.shape, BF16),
            vmem(w_key.shape, BF16),
            vmem(w_value.shape, BF16),
            vmem((2, nq, BLK, 2 * HD), BF16),
            vmem((nh, nb, W, 2 * HD), BF16),
            vmem((nh, n_rows, 2 * HD), BF16),
            vmem((n_rows, slots), BF16),
            vmem((nb * W, slots), BF16),
            vmem((nh, n_rows, 128), F32),
            vmem((nh, n_rows, 128), F32),
            vmem((nh, nz, out_rows // 2, 2 * HD), BF16),
            vmem((nh, nz, out_rows // 2, 2 * HD), BF16),
            vmem((nz,) + w_out.shape, BF16),
            vmem((out_rows, w_out.shape[1]), F32),
            dma((8,)),
            dma((nh, nb // 2)),
            dma((nh, nb // 2)),
            dma((nh, nb)),
            dma((nh, nz)),
            dma((nh, nz)),
            dma((nz,)),
            dma((nz, nt)),
            dma((nz, nt)),
            dma((nz, 2 * nt)),
        ],
        compiler_params=pltpu.CompilerParams(
            collective_id=0, has_side_effects=True, vmem_limit_bytes=53 * MIB
        ),
        name="layer",
    )(block_mask, tokens.reshape(nq, BLK, width), w_query, w_key, w_value, w_out)


def solution(mesh):
    return jax.shard_map(
        functools.partial(on_device, mesh.shape["tiles"], mesh.shape["band"], mesh.shape["head"]),
        mesh=mesh,
        in_specs=(
            P(("tiles", "band"), None),
            P(None, "head"),
            P(None, "head"),
            P(None, "head"),
            P("head", None),
            P("tiles", None),
        ),
        out_specs=P(("tiles", "band", "head"), None),
        check_vma=False,
    )
```

```python
import functools
import jax
import jax.numpy as jnp
from jax import lax
from jax.experimental import pallas as pl
from jax.experimental.pallas import tpu as pltpu
from jax.sharding import PartitionSpec as P

HD = 64
BLK = 128
KEEP = 6
LOW = -float(2**100)
SCALE = HD**-0.5 * 1.4426950408889634
MIB = 1 << 20
BF16 = jnp.bfloat16
F32 = jnp.float32
I32 = jnp.int32
NT = (((1,), (1,)), ((), ()))
W = KEEP * BLK


def select_blocks(mask, me, per_band):
    named = []
    for i in range(per_band):
        named.append(
            functools.reduce(jnp.maximum, [mask[r, me * per_band + i] for r in range(mask.shape[0])])
        )
    picks, rank = [0] * KEEP, 0
    for i in range(per_band):
        for k in range(min(i + 1, KEEP)):
            picks[k] = picks[k] + i * named[i] * (rank == k)
        rank = rank + named[i]
    return picks


def make_bias(mask, me, nb, bias):
    n_rows, n_kb = mask.shape
    nq = n_kb // nb
    slots = bias.shape[1]
    everything = mask[...].astype(F32).T
    rows = mask[pl.ds(pl.multiple_of(me * nq, nq), nq), :].astype(F32)
    named = jnp.broadcast_to(jnp.max(everything, axis=1, keepdims=True), (n_kb, slots))
    left = lax.broadcasted_iota(I32, (n_kb, n_kb), 0)
    right = lax.broadcasted_iota(I32, (n_kb, n_kb), 1)
    earlier = ((right < left) & (left // nq == right // nq)).astype(F32)
    rank = jnp.dot(earlier, named, preferred_element_type=F32)
    band = (lax.broadcasted_iota(I32, (n_kb, slots), 0) // nq).astype(F32)
    slot = lax.broadcasted_iota(I32, (n_kb, slots), 1).astype(F32)
    place = jnp.where((slot == band * KEEP + rank) & (named > 0) & (rank < KEEP), 1.0, 0.0)
    allowed = jnp.dot(rows, place, preferred_element_type=F32)
    value = jnp.where(allowed > 0, 0.0, LOW)
    for i in range(nq):
        bias[i * BLK : (i + 1) * BLK, :] = jnp.broadcast_to(value[i : i + 1, :], (BLK, slots)).astype(BF16)


def layer(
    nt, nb, nz, mask_h, tok_h, wq_h, wk_h, wv_h, wo_h, out,
    mask_s, mask_v, tok, wq, wk, wv, made, kv, q_pad, bias, onehot, top, acc, att, got, wo, pre,
    load, kv_send, kv_fwd, kv_recv, a_send, a_recv, w1_send, w2_send, w3_send, w_recv,
):
    nh = q_pad.shape[0]
    nq = tok.shape[0]
    n_chips = nb // 2
    slots = bias.shape[1]
    n_rows = nq * BLK
    depth = wo.shape[1]
    parts = 2 * nt
    per_part = depth // parts
    half = att.shape[2]
    tile, band, z = lax.axis_index("tiles"), lax.axis_index("band"), lax.axis_index("head")
    chip, core = band // 2, lax.rem(band, 2)
    sibling = chip * 2 + 1 - core
    mesh_id = pl.DeviceIdType.MESH

    pairs = ((mask_h, mask_s), (mask_h, mask_v), (wk_h, wk), (wv_h, wv),
             (tok_h.at[: nq // 2], tok.at[: nq // 2]), (tok_h.at[nq // 2 :], tok.at[nq // 2 :]),
             (wq_h, wq), (wo_h, wo.at[z]))
    loads = [pltpu.make_async_copy(a, b, load.at[i]) for i, (a, b) in enumerate(pairs)]
    def chip_at(step):
        return lax.rem(chip + step, n_chips)

    peers = [{"band": sibling}]
    peers += [{"band": chip_at(d) * 2 + core} for d in range(1, n_chips)]
    peers += [{"head": lax.rem(z + d, nz)} for d in range(1, nz)]
    peers += [{"tiles": lax.rem(tile + d, nt)} for d in range(1, nt)]
    barrier = pltpu.get_barrier_semaphore()
    for p in peers:
        pl.semaphore_signal(barrier, inc=1, device_id=p, device_id_type=mesh_id)
    for c in loads:
        c.start()

    def remote(src, dst, send, recv, to):
        return pltpu.make_async_remote_copy(
            src_ref=src, dst_ref=dst, send_sem=send, recv_sem=recv, device_id=to, device_id_type=mesh_id
        )

    def kv_copy(h, origin, send, to):
        return remote(kv.at[h, origin], kv.at[h, origin], send, kv_recv.at[h, origin], {"band": to})

    def kv_direct(h, step):
        return kv_copy(h, band, kv_send.at[h, step], chip_at(step) * 2 + core)

    def kv_own(h):
        return kv_copy(h, band, kv_send.at[h, 0], sibling)

    def kv_forward(h, step):
        return kv_copy(h, chip_at(step) * 2 + core, kv_fwd.at[h, step], sibling)

    def kv_arrived(h, origin):
        kv_copy(h, origin, kv_recv.at[h, origin], sibling).wait_recv()

    def w_piece(source, part):
        return wo.at[source, pl.ds(pl.multiple_of(part * per_part, per_part), per_part)]

    my_part = tile * 2 + core

    def w_first(d):
        here = pl.ds(pl.multiple_of(my_part * per_part, per_part), per_part)
        return remote(
            wo_h.at[here], w_piece(z, my_part), w1_send.at[d], w_recv.at[z, my_part], {"head": lax.rem(z + d, nz)}
        )

    def w_second(d, t):
        source = lax.rem(z + d, nz)
        piece = w_piece(source, my_part)
        return remote(piece, piece, w2_send.at[d, t], w_recv.at[source, my_part], {"tiles": lax.rem(tile + t, nt)})

    def w_third(d, t):
        source, part = lax.rem(z + d, nz), lax.rem(tile + t, nt) * 2 + core
        piece = w_piece(source, part)
        return remote(piece, piece, w3_send.at[d, t], w_recv.at[source, part], {"band": sibling})

    def w_arrived(d, part):
        source = lax.rem(z + d, nz)
        piece = w_piece(source, part)
        remote(piece, piece, w1_send.at[d], w_recv.at[source, part], {"band": sibling}).wait_recv()

    loads[0].wait()
    sel = select_blocks(mask_s, band, nq)
    pl.semaphore_wait(barrier, len(peers))
    for d in range(1, nz):
        w_first(d).start()

    lane = lax.broadcasted_iota(I32, (1, BLK), 1)
    low_half = lane < HD

    loads[2].wait()
    loads[3].wait()
    for g in range(0, nh, 2):
        cols = slice(g * HD, (g + 2) * HD)
        weight = jnp.concatenate([wk[:, cols], wv[:, cols]], axis=1)
        for i in range(2):
            blocks = slice(i * nq // 2, (i + 1) * nq // 2)
            if g == 0:
                loads[4 + i].wait()
            both = jnp.dot(tok[blocks].reshape(n_rows // 2, -1), weight, preferred_element_type=F32)
            keys, vals = both[:, :BLK], both[:, BLK:]
            one = jnp.where(low_half, keys, pltpu.roll(vals, HD, 1)).astype(BF16)
            two = jnp.where(low_half, pltpu.roll(keys, HD, 1), vals).astype(BF16)
            made[0, blocks] = one.reshape(nq // 2, BLK, BLK)
            made[1, blocks] = two.reshape(nq // 2, BLK, BLK)
        for h in range(2):
            for k in range(KEEP):
                kv[g + h, band, k * BLK : (k + 1) * BLK, :] = made[h, sel[k]]
        for h in (g, g + 1):
            if h < 2:
                for d in range(1, n_chips):
                    kv_direct(h, d).start()
            kv_own(h).start()

    loads[6].wait()
    queries = jnp.dot(tok[...].reshape(n_rows, -1), wq[...], preferred_element_type=F32) * SCALE
    for h in range(nh):
        two = queries[:, (h // 2) * BLK : (h // 2 + 1) * BLK]
        if h % 2:
            two = pltpu.roll(two, HD, 1)
        q_pad[h] = jnp.where(low_half, two, 0.0).astype(BF16)

    slot_of = lax.broadcasted_iota(I32, (BLK, slots), 1)
    for s in range(nb * KEEP):
        onehot[s * BLK : (s + 1) * BLK, :] = jnp.where(slot_of == s, 1.0, 0.0).astype(BF16)
    loads[1].wait()
    make_bias(mask_v, band, nb, bias)
    tq = n_rows // 2
    far = (z * 2) // nz

    def part(i):
        return pl.ds(pl.multiple_of(lax.rem(i + 1 + far, 2) * tq, tq), tq)

    def span(b):
        return pl.ds(pl.multiple_of(b * W, W), W)

    def score(h, b, i):
        r = part(i)
        q = jnp.concatenate([q_pad[h, r, :], bias[r, :]], axis=1)
        k = jnp.concatenate([kv[h, b], onehot[span(b), :]], axis=1)
        return lax.dot_general(q, k, NT, preferred_element_type=F32)

    def gather(s, h, b, i, first):
        r = part(i)
        cut = [s[:, j * BLK : (j + 1) * BLK] for j in range(KEEP)]
        m = jnp.broadcast_to(functools.reduce(jnp.maximum, cut).max(axis=1, keepdims=True), (tq, BLK))
        if not first:
            before = top[h, r, :]
            m = jnp.maximum(before, m)
        top[h, r, :] = m
        p = jnp.concatenate([jnp.exp2((x - m).astype(BF16)) for x in cut], axis=1)
        tile_kv = kv[h, b]
        v = jnp.where(low_half, jnp.ones_like(tile_kv), tile_kv)
        a = jnp.dot(p, v, preferred_element_type=F32)
        if not first:
            a = a + acc[h, r, :] * jnp.exp2(before - m)
        acc[h, r, :] = a

    def block(h, bands, first, done=None):
        units = [(b, i, first and n == 0) for n, b in enumerate(bands) for i in range(2)]
        s = score(h, *units[0][:2])
        for n, (b, i, start) in enumerate(units):
            after = score(h, *units[n + 1][:2]) if n + 1 < len(units) else None
            gather(s, h, b, i, start)
            if done is not None:
                done(i)
            s = after

    def local_block(h, _):
        @pl.when((h >= 1) & (h + 1 < nh))
        def _():
            for d in range(1, n_chips):
                kv_direct(h + 1, d).start()

        kv_arrived(h, sibling)
        block(h, (band, sibling), True)
        return 0

    def a_copy(h, d):
        to = lax.rem(z + d, nz)
        return remote(att.at[h, to], got.at[h, z], a_send.at[h, d], a_recv.at[h, z], {"head": to})

    def a_arrived(h, d):
        origin = lax.rem(z + d, nz)
        remote(att.at[h, origin], got.at[h, origin], a_send.at[h, d], a_recv.at[h, origin], {"head": origin}).wait_recv()

    reach = nz // 2

    def finish(h, i):
        base = lax.rem(far + 1 + i, 2) * reach
        order = [lax.rem(z + e, reach) + base for e in range(reach)]
        for p in order:
            lo = p * 2 * half
            a0 = acc[h, pl.ds(pl.multiple_of(lo, half), half), :]
            a1 = acc[h, pl.ds(pl.multiple_of(lo + half, half), half), :]
            value = jnp.where(low_half, pltpu.roll(a0, HD, 1), a1)
            mass = jnp.where(low_half, a0, pltpu.roll(a1, HD, 1))
            att[h, p] = (value / mass).astype(BF16)

    def far_block(h, _):
        @pl.when(h == 1)
        def _():
            for d in range(1, nz):
                w_arrived(d, my_part)
                for t in range(nt):
                    (w_second(d, t) if t else w_third(d, 0)).start()

        for d in range(1, n_chips):
            same = chip_at(d) * 2 + core
            kv_arrived(h, same)
            kv_forward(h, d).start()
            block(h, (same,), False)
            kv_arrived(h, chip_at(d) * 2 + 1 - core)
            block(h, (chip_at(d) * 2 + 1 - core,), False, functools.partial(finish, h) if d == n_chips - 1 else None)
        for d in range(1, nz):
            a_copy(h, d).start()
        got[h, z] = att[h, z]
        return 0

    def turn(i, _):
        @pl.when(i < nh)
        def _():
            local_block(i, 0)

        @pl.when(i >= 2)
        def _():
            far_block(i - 2, 0)

        return 0

    lax.fori_loop(0, nh + 2, turn, 0)

    for t in range(1, nt):
        for d in range(1, nz):
            w_arrived(d, lax.rem(tile + t, nt) * 2 + core)
            w_third(d, t).start()
    for t in range(nt):
        for d in range(1, nz):
            w_arrived(d, lax.rem(tile + t, nt) * 2 + 1 - core)
    loads[7].wait()

    def heads(hs):
        return jnp.concatenate(
            [
                jnp.concatenate([got[h, s][:, r * HD : (r + 1) * HD] for s in range(nz) for h in hs], axis=1)
                for r in range(2)
            ],
            axis=0,
        )

    def weights(hs):
        return jnp.concatenate([wo[s, hs[0] * HD : (hs[-1] + 1) * HD, :] for s in range(nz)], axis=0)

    early, last = list(range(nh - 1)), [nh - 1]
    for h in early:
        for d in range(1, nz):
            a_arrived(h, d)
    pre[...] = jnp.dot(heads(early), weights(early), preferred_element_type=F32)
    for d in range(1, nz):
        a_arrived(nh - 1, d)
    out[...] = (pre[...] + jnp.dot(heads(last), weights(last), preferred_element_type=F32)).astype(BF16)

    for h in range(nh):
        kv_own(h).wait_send()
        for d in range(1, n_chips):
            kv_direct(h, d).wait_send()
            kv_forward(h, d).wait_send()
        for d in range(1, nz):
            a_copy(h, d).wait_send()
    for d in range(1, nz):
        w_first(d).wait_send()
        for t in range(nt):
            w_third(d, t).wait_send()
            if t:
                w_second(d, t).wait_send()


def on_device(nt, nb, nz, tokens, w_query, w_key, w_value, w_out, block_mask):
    nh = w_query.shape[1] // HD
    n_rows, width = tokens.shape
    nq = n_rows // BLK
    out_rows = n_rows // nz
    slots = -(-nb * KEEP // 128) * 128
    hbm = pl.BlockSpec(memory_space=pltpu.HBM)
    vmem = pltpu.VMEM
    dma = pltpu.SemaphoreType.DMA
    return pl.pallas_call(
        functools.partial(layer, nt, nb, nz),
        out_shape=jax.ShapeDtypeStruct((out_rows, w_out.shape[1]), BF16),
        in_specs=[hbm] * 6,
        out_specs=pl.BlockSpec(memory_space=pltpu.VMEM),
        scratch_shapes=[
            pltpu.SMEM(block_mask.shape, I32),
            vmem(block_mask.shape, I32),
            vmem((nq, BLK, width), BF16),
            vmem(w_query.shape, BF16),
            vmem(w_key.shape, BF16),
            vmem(w_value.shape, BF16),
            vmem((2, nq, BLK, 2 * HD), BF16),
            vmem((nh, nb, W, 2 * HD), BF16),
            vmem((nh, n_rows, 2 * HD), BF16),
            vmem((n_rows, slots), BF16),
            vmem((nb * W, slots), BF16),
            vmem((nh, n_rows, 128), F32),
            vmem((nh, n_rows, 128), F32),
            vmem((nh, nz, out_rows // 2, 2 * HD), BF16),
            vmem((nh, nz, out_rows // 2, 2 * HD), BF16),
            vmem((nz,) + w_out.shape, BF16),
            vmem((out_rows, w_out.shape[1]), F32),
            dma((8,)),
            dma((nh, nb // 2)),
            dma((nh, nb // 2)),
            dma((nh, nb)),
            dma((nh, nz)),
            dma((nh, nz)),
            dma((nz,)),
            dma((nz, nt)),
            dma((nz, nt)),
            dma((nz, 2 * nt)),
        ],
        compiler_params=pltpu.CompilerParams(
            collective_id=0, has_side_effects=True, vmem_limit_bytes=53 * MIB
        ),
        name="layer",
    )(block_mask, tokens.reshape(nq, BLK, width), w_query, w_key, w_value, w_out)


def solution(mesh):
    return jax.shard_map(
        functools.partial(on_device, mesh.shape["tiles"], mesh.shape["band"], mesh.shape["head"]),
        mesh=mesh,
        in_specs=(
            P(("tiles", "band"), None),
            P(None, "head"),
            P(None, "head"),
            P(None, "head"),
            P("head", None),
            P("tiles", None),
        ),
        out_specs=P(("tiles", "band", "head"), None),
        check_vma=False,
    )
```
